32 devices in a mesh: pipe: 8 (over y, x, core), seq: 4 (over z).
Axes of the slice: x: 2, y: 2, z: 4, core: 2. Of those that a mesh axis runs over, the one named last changes fastest.
Arguments:
- activations: bfloat16 [512, 4096], P('seq', 'pipe'), may hold values from -6 to 6
- norm_gain: bfloat16 [4096], P('pipe'), may hold values from 0.5 to 2
- w_qkv: bfloat16 [8, 4096, 384], P('pipe', 'seq'), may hold values from -1 to 1
- w_out: bfloat16 [8, 128, 4096], P('pipe', None, 'seq'), may hold values from -0.375 to 0.375
- block_mask: int32 [4, 4], replicated, may hold values from 0 to 1, as said below
- cotangent: bfloat16 [512, 4096], P('seq', 'pipe'), may hold values from -6 to 6
Outputs:
- output: bfloat16 [512, 4096], P('seq', 'pipe')
- input_grad: bfloat16 [512, 4096], P('seq', 'pipe')
The draws below stay inside these ranges and needn't reach their ends.
Inputs may be any that keep to these rules, and one draw needn't show every extreme that they name: `block_mask`: every diagonal entry is 1; the rows hold uneven numbers of ones.
All inputs are finite; a program needn't handle non-finite values.
Results may differ from the reference program's by a relative error of at most 0.02.
The reference program's roundings to bfloat16 on the way count: a program that leaves them out, or rounds other values in their place, can miss the bound.
Values may be sent and summed in bfloat16 or wider, within the bound.
No kernel may reach another device: no remote copies, remote signals or barrier semaphores. Data moves between devices by JAX's collectives and lax.ppermute only.
A program may use at most 64 MiB of HBM per device.

```python
import math
import jax
import jax.numpy as jnp
from jax import lax

D = 4096
HD = 128
BLOCK = 128
HEADS = 8
TOKENS = 512
NB = 4


def draw_w_qkv(key, part):
    key = jax.random.fold_in(key, 11)
    shape = (HEADS, D, 3 * HD)
    spread = 2.0 / math.sqrt(D)
    return jnp.clip(jnp.clip(jax.random.normal(key, shape, jnp.float32), -6.0, 6.0) * spread, -1.0, 1.0).astype(jnp.bfloat16)


def draw_block_mask(key, part):
    key = jax.random.fold_in(key, 7)
    first, second = jax.random.split(key)
    levels = jax.random.randint(first, (NB, 1), 1, 9)
    draws = jax.random.randint(second, (NB, NB), 0, 8)
    diagonal = jnp.arange(NB)[:, None] == jnp.arange(NB)[None, :]
    return jnp.where((draws < levels) | diagonal, 1, 0).astype(jnp.int32)


def level_of(own_key, dims, pieces, least, top_value):
    level = 1.0
    for dim, parts in pieces:
        steps = jax.random.uniform(jax.random.fold_in(jax.random.fold_in(own_key, 6), dim), (parts,), jnp.float32, least / len(pieces), top_value / len(pieces))
        level = level * jnp.repeat(jnp.exp(steps), dims[dim] // parts).reshape((-1,) + (1,) * (len(dims) - 1 - dim))
    return level


def centred(key, shape, scale, most, pieces=(), held_as=jnp.bfloat16):
    drawn = scale * jax.random.normal(key, shape, jnp.float32)
    if pieces:
        drawn = drawn * level_of(key, shape, pieces, -0.22, 0.18)
    return jnp.clip(drawn, -most, most).astype(held_as)


def setup_inputs(seed: int = 0) -> dict:
    streams_of = jax.random.split(jax.random.key(seed), 7)
    activations = centred(streams_of[0], (TOKENS, D), 1.0, 6.0, ((0, 4), (1, 8)))
    norm_gain = jnp.clip(jnp.exp(math.log(2.0) - 1.3862944 * jax.random.uniform(streams_of[1], (D,), jnp.float32) ** level_of(streams_of[1], (D,), ((0, 8),), -0.2, 0.2)), 0.5, 2.0).astype(jnp.bfloat16)
    w_qkv = draw_w_qkv(jax.random.fold_in(streams_of[6], 71), 0)
    w_out = centred(streams_of[3], (HEADS, HD, D), (HEADS * HD // 4) ** -0.5, 0.375, ((0, 8), (2, 4)))
    block_mask = draw_block_mask(jax.random.fold_in(streams_of[6], 71), 0)
    cotangent = centred(streams_of[5], (TOKENS, D), 1.0, 6.0, ((0, 4), (1, 8)))
    return dict(activations=activations, norm_gain=norm_gain, w_qkv=w_qkv, w_out=w_out, block_mask=block_mask, cotangent=cotangent)


def reference(activations, norm_gain, w_qkv, w_out, block_mask, cotangent):
    input_rows = activations.astype(jnp.float32)
    square_root_norm = lax.rsqrt(lax.optimization_barrier(jnp.mean(input_rows * input_rows, axis=-1, keepdims=True)) + 1e-05)
    gain = norm_gain.astype(jnp.float32)
    normed = (input_rows * square_root_norm * gain).astype(jnp.bfloat16)
    normalized_input = input_rows * square_root_norm
    factor = 1.0 / math.sqrt(HD)
    allowed = jnp.repeat(jnp.repeat(block_mask, BLOCK, axis=0), BLOCK, axis=1) > 0
    grad_in = cotangent

    def per_head(carry, weights):
        out_sum, grad_sum = carry
        w_head, wo_head = weights
        projected = jnp.dot(normed, w_head, preferred_element_type=jnp.float32)
        query = projected[:, :HD].astype(jnp.bfloat16)
        key_part = projected[:, HD:2 * HD].astype(jnp.bfloat16)
        value = projected[:, 2 * HD:].astype(jnp.bfloat16)
        scores = jnp.dot(query, key_part.T, preferred_element_type=jnp.float32) * factor
        scores = jnp.where(allowed, scores, -1e+30)
        top = lax.optimization_barrier(jnp.max(scores, axis=-1, keepdims=True))
        expd = jnp.where(allowed, jnp.exp(scores - top), 0.0)
        probs = expd / lax.optimization_barrier(jnp.sum(expd, axis=-1, keepdims=True))
        probs_round = probs.astype(jnp.bfloat16)
        attended = jnp.dot(probs_round, value, preferred_element_type=jnp.float32).astype(jnp.bfloat16)
        term = jnp.dot(attended, wo_head, preferred_element_type=jnp.float32).astype(jnp.bfloat16)
        out_sum = out_sum + term.astype(jnp.float32)
        d_att = jnp.dot(grad_in, wo_head.T, preferred_element_type=jnp.float32).astype(jnp.bfloat16)
        d_probs = jnp.dot(d_att, value.T, preferred_element_type=jnp.float32)
        delta = lax.optimization_barrier(jnp.sum(probs * d_probs, axis=-1, keepdims=True))
        d_scores = (probs * (d_probs - delta) * factor).astype(jnp.bfloat16)
        d_query = jnp.dot(d_scores, key_part, preferred_element_type=jnp.float32).astype(jnp.bfloat16)
        d_key = jnp.dot(d_scores.T, query, preferred_element_type=jnp.float32).astype(jnp.bfloat16)
        d_value = jnp.dot(probs_round.T, d_att, preferred_element_type=jnp.float32).astype(jnp.bfloat16)
        d_proj = jnp.concatenate([d_query, d_key, d_value], axis=1)
        d_normed = jnp.dot(d_proj, w_head.T, preferred_element_type=jnp.float32)
        rescaled_values = d_normed * gain
        gradient_component = (square_root_norm * (rescaled_values - normalized_input * lax.optimization_barrier(jnp.mean(rescaled_values * normalized_input, axis=-1, keepdims=True)))).astype(jnp.bfloat16)
        grad_sum = grad_sum + gradient_component.astype(jnp.float32)
        return ((out_sum, grad_sum), None)
    start = jnp.zeros(input_rows.shape, jnp.float32)
    (out_sum, grad_sum), unused = lax.scan(per_head, (start, start), (w_qkv, w_out))
    output = (input_rows + out_sum).astype(jnp.bfloat16)
    input_grad = (cotangent.astype(jnp.float32) + grad_sum).astype(jnp.bfloat16)
    return (output, input_grad)
```

```python
import functools
import math

import jax
import jax.numpy as jnp
from jax import lax
from jax.experimental import pallas as pl
from jax.experimental.pallas import tpu as pltpu
from jax.sharding import PartitionSpec as P

EPS = 1e-05
VMEM_LIMIT = 48 * 1024 * 1024
STAT = 128
AXES = ("pipe", "seq")
F32 = jnp.float32
BF16 = jnp.bfloat16


def place():
    pipe = lax.axis_index("pipe")
    return pipe // 2, pipe % 2, lax.axis_index("seq")


def nt(a, b):
    return lax.dot_general(a, b, (((1,), (1,)), ((), ())), preferred_element_type=F32)


def tn(a, b):
    return lax.dot_general(a, b, (((0,), (0,)), ((), ())), preferred_element_type=F32)


def nn(a, b):
    return jnp.dot(a, b, preferred_element_type=F32)


def span(index, size):
    if isinstance(index, int):
        return pl.ds(index * size, size)
    return pl.ds(pl.multiple_of(index * size, size), size)


def call(kernel, out_shape, *args, scratch=(), smem=()):
    specs = [
        pl.BlockSpec(memory_space=pltpu.SMEM if i in smem else pltpu.VMEM) for i in range(len(args))
    ]
    return pl.pallas_call(
        kernel,
        out_shape=out_shape,
        in_specs=specs,
        out_specs=jax.tree.map(lambda _: pl.BlockSpec(memory_space=pltpu.VMEM), out_shape),
        scratch_shapes=list(scratch),
        compiler_params=pltpu.CompilerParams(vmem_limit_bytes=VMEM_LIMIT),
    )(*args)


def shape(*dims, dtype=BF16):
    return jax.ShapeDtypeStruct(dims, dtype)


def each(n, body):
    if n <= 4:
        for e in range(n):
            body(e)
    else:
        lax.fori_loop(0, n, lambda e, carry: (body(e), carry)[1], 0)


def stack_kernel(own, sib, out):
    _, core, _ = place()
    rows, feats = own.shape[0], out.shape[1]
    out[:rows, :] = own[:, span(core, feats)]
    out[rows:, :] = sib[:, span(core, feats)]


def rows_kernel(x, gain, out):
    rows, feats = x.shape
    out[:rows, :] = x[...]
    out[rows:, :] = jnp.broadcast_to(gain[...], (16, feats))


def project_kernel(n, w, *refs):
    same, sib, outs = refs[:n], refs[n : 2 * n], refs[2 * n : 3 * n]
    own_squares, high, low, held, held_squares = refs[3 * n :]
    chip, core, plane = place()
    feats = same[0].shape[1]
    rows = same[0].shape[0] - 16
    width = w.shape[1]
    ones = jnp.ones((8, feats), BF16)
    line = lax.broadcasted_iota(jnp.int32, (16, rows), 0)

    def parts(value):
        first = value.astype(BF16)
        return first, (value - first.astype(F32)).astype(BF16)

    total = jnp.zeros((n * rows, width), F32)
    def gain_of(blocks):
        chosen = jnp.zeros((8, feats), F32)
        for d in range(n):
            lines = blocks[d][rows:, :].astype(F32)[:8]
            chosen += jnp.where(jnp.bitwise_xor(chip, d) == plane, lines, 0.0)
        return chosen[0:1, :]

    gains = gain_of(same), gain_of(sib)
    for d in range(n):
        slot = jnp.bitwise_xor(chip, d)
        squares = jnp.zeros((8, rows), F32)
        for i, blocks in enumerate((same, sib)):
            values = blocks[d][:rows, :].astype(F32)
            at = (span(slot, rows), slice(i * feats, (i + 1) * feats))
            high[at], low[at] = parts(values * gains[i])
            square_high, square_low = parts(values * values)
            squares += nt(ones, square_high) + nt(ones, square_low)
        held_squares[slot] = squares
    w_same, w_sib = w[span(core, feats), :], w[span(1 - core, feats), :]
    product = nn(high[:, :feats], w_same) + nn(low[:, :feats], w_same)
    product += nn(high[:, feats:], w_sib) + nn(low[:, feats:], w_sib)
    held[...] = product
    outs[0][...] = held[:rows, :]
    own_squares[...] = held_squares[0]
    for e in range(1, n):
        outs[e][:rows, :] = held[e * rows : (e + 1) * rows, :].astype(BF16)
        squares = held_squares[e][0:1, :]
        first = squares.astype(BF16).astype(F32)
        stat = jnp.where(line == 0, first, jnp.where(line == 1, squares - first, 0.0))
        outs[e][rows:, :] = jnp.zeros((16, width), BF16)
        outs[e][rows:, :rows] = stat.astype(BF16)


def combine_kernel(n, features, squares, d_att, d_att_sib, *refs):
    parts, (out, root) = refs[:n], refs[n:]
    rows, width = parts[0].shape
    total = parts[0][...]
    sums = squares[0:1, :]
    for part in parts[1:]:
        total += part[:rows, :].astype(F32)
        sums += jnp.sum(part[rows:, :rows].astype(F32), axis=0, keepdims=True)
    scale = jnp.broadcast_to(lax.rsqrt(sums / features + EPS), (rows, rows)).T
    root[...] = scale
    out[:, :width] = (total * scale[:, :1]).astype(BF16)
    out[:, width:] = (d_att[...] + d_att_sib[...]).astype(BF16)


def cotangent_kernel(n, *refs):
    cots, weights, (own, sib, held) = refs[:n], refs[n : 2 * n], refs[2 * n :]
    chip, _, plane = place()
    turn = jnp.bitwise_xor(chip, plane)
    rows, head = own.shape
    for d in range(n):
        held[jnp.bitwise_xor(turn, d)] = cots[d][...]
    total = jnp.zeros((rows, 2 * head), F32)
    for e in range(n):
        total += nt(held[e], weights[e][...])
    own[...] = total[:, :head]
    sib[...] = total[:, head:]


def split_stat(column):
    high = column.astype(BF16).astype(F32)
    lane = lax.broadcasted_iota(jnp.int32, (column.shape[0], STAT), 1)
    return jnp.where(lane == 0, high, jnp.where(lane == 1, column - high, 0.0)).astype(BF16)


def attention_kernel(n, features, mask, *refs):
    blocks = refs[:n]
    attended_out, d_proj, held, probs_held, d_scores_held = refs[n:]
    _, _, plane = place()
    rows = blocks[0].shape[0]
    head = blocks[0].shape[1] // 4
    factor = 1.0 / math.sqrt(head)
    for e in range(n):
        held[e * rows : (e + 1) * rows, :] = blocks[e][...]
    key = held[:, head : 2 * head]
    value = held[:, 2 * head : 3 * head]
    column_block = lax.broadcasted_iota(jnp.int32, (1, n * rows), 1) // rows

    def one_block(e):
        at = span(e, rows)
        row_plane = jnp.bitwise_xor(plane, e)
        allowed = jnp.zeros((1, n * rows), jnp.int32)
        for other in range(n):
            entry = mask[row_plane, jnp.bitwise_xor(plane, other)]
            allowed = jnp.where(column_block == other, entry, allowed)
        scores = jnp.where(allowed > 0, nt(held[at, :head], key) * factor, -1e30)
        expd = jnp.exp(scores - jnp.max(scores, axis=-1, keepdims=True))
        probs = expd / jnp.sum(expd, axis=-1, keepdims=True)
        probs_round = probs.astype(BF16)
        d_probs = nt(held[at, 3 * head :], value)
        delta = jnp.sum(probs * d_probs, axis=-1, keepdims=True)
        d_scores = (probs * (d_probs - delta) * factor).astype(BF16)
        d_proj[at, :head] = nn(d_scores, key).astype(BF16)
        probs_held[at, :] = probs_round
        d_scores_held[at, :] = d_scores

    each(n, one_block)
    d_proj[:, head : 2 * head] = tn(d_scores_held[...], held[:, :head]).astype(BF16)
    d_proj[:, 2 * head :] = tn(probs_held[...], held[:, 3 * head :]).astype(BF16)
    attended_out[:, :head] = nn(probs_held[:rows, :], value).astype(BF16)
    products = d_proj[:rows, :].astype(F32) * held[:rows, : 3 * head].astype(F32)
    mean = jnp.sum(products, axis=1, keepdims=True) / features
    attended_out[:, head:] = split_stat(mean)


def back_own_kernel(d_proj, w, out):
    _, core, _ = place()
    out[...] = nt(d_proj[...], w[span(core, out.shape[1]), :])


def back_sum_kernel(n, own, d_proj, w, *refs):
    outs, held = refs[:n], refs[n]
    chip, core, _ = place()
    rows, feats = outs[0].shape
    held[...] = (own[...] + nt(d_proj[...], w[span(core, feats), :])).astype(BF16)
    for d in range(n):
        outs[d][...] = held[span(jnp.bitwise_xor(chip, d), rows), :]


def term_kernel(n, own, sib, *refs):
    weights, outs, held = refs[:n], refs[n : 2 * n], refs[2 * n]
    chip, _, plane = place()
    turn = jnp.bitwise_xor(chip, plane)
    head = weights[0].shape[0] // 2
    feats = weights[0].shape[1]
    for e in range(n):
        term = nn(own[:, :head], weights[e][:head, :]) + nn(sib[:, :head], weights[e][head:, :])
        held[jnp.bitwise_xor(turn, e)] = term.astype(BF16)
    means = own[:, head:].astype(F32) + sib[:, head:].astype(F32)
    stat = split_stat(jnp.sum(means, axis=1, keepdims=True))
    for d in range(n):
        outs[d][:, :feats] = held[d]
        outs[d][:, feats:] = stat


def sum_kernel(n, *refs):
    total = refs[0][...].astype(F32)
    for part in refs[1:n]:
        total += part[...].astype(F32)
    refs[n][...] = total.astype(BF16)


def finish_output_kernel(n, x, *refs):
    parts, (out, mean) = refs[:n], refs[n:]
    feats = x.shape[1]
    total = parts[0][...].astype(F32)
    for part in parts[1:]:
        total += part[...].astype(F32)
    out[...] = (x[...].astype(F32) + total[:, :feats]).astype(BF16)
    mean[...] = jnp.broadcast_to(jnp.sum(total[:, feats:], axis=1, keepdims=True), mean.shape)


def finish_grad_kernel(x, gain, cot, root, mean, grad, out):
    scale = root[:, :1]
    shift = scale * mean[:, :1]
    centred = grad[...].astype(F32) * gain[...].astype(F32) - x[...].astype(F32) * shift
    out[...] = (cot[...].astype(F32) + scale * centred).astype(BF16)


def per_device(n, activations, norm_gain, w_qkv, w_out, block_mask, cotangent):
    rows, feats = activations.shape
    features = feats * 2 * n
    head = w_out.shape[1]
    width = w_qkv.shape[2]
    tokens = n * rows

    def move(value, target):
        pairs = []
        for chip in range(n):
            for core in range(2):
                for plane in range(n):
                    to_chip, to_core, to_plane = target(chip, core, plane)
                    pairs.append(((2 * chip + core) * n + plane, (2 * to_chip + to_core) * n + to_plane))
        return lax.ppermute(value, AXES, pairs)

    def swap(value):
        return move(value, lambda c, k, z: (c, 1 - k, z))

    def to_chip(value, d):
        return move(value, lambda c, k, z: (c ^ d, k, z))

    def to_plane(value, e):
        return move(value, lambda c, k, z: (c, k, z ^ e))

    def after(value, *earlier):
        return lax.optimization_barrier((value, *earlier))[0]

    w = w_qkv[0]
    wo = w_out[0]

    x_held = move(activations, lambda c, k, z: (z ^ c, k, c))
    gain = norm_gain.reshape(1, feats)
    wo_sib = swap(wo)
    cots = [cotangent] + [to_chip(cotangent, d) for d in range(1, n)]
    own = call(stack_kernel, shape(2 * head, feats), wo, wo_sib)
    order, step = [0, n // 2], n // 2
    far = to_plane(own, step)
    x_held, *cots = lax.optimization_barrier((x_held, *cots))
    x_held = call(rows_kernel, shape(rows + 16, feats), x_held, gain)
    x_same, x_sib = [x_held], [swap(x_held)]
    for d in range(1, n):
        block = to_chip(x_held, d)
        if d == min(3, n - 1):
            block, far = lax.optimization_barrier((block, far))
        x_same.append(block)
        x_sib.append(swap(block))
    weights = [own, far]
    while step > 1:
        step //= 2
        ready = [after(part, x_sib[0 if i == 0 else 0]) for i, part in enumerate(weights)]
        weights += [to_plane(part, step) for part in ready]
        order += [o ^ step for o in order]
    *parts, own_squares = call(
        functools.partial(project_kernel, n),
        [shape(rows, width, dtype=F32)]
        + [shape(rows + 16, width)] * (n - 1)
        + [shape(8, rows, dtype=F32)],
        w, *x_same, *x_sib,
        scratch=[
            pltpu.VMEM((n * rows, 2 * feats), BF16),
            pltpu.VMEM((n * rows, 2 * feats), BF16),
            pltpu.VMEM((n * rows, width), F32),
            pltpu.VMEM((n, 8, rows), F32),
        ],
    )
    parts = [parts[0]] + [to_plane(parts[e], e) for e in range(1, n)]

    weights = [weights[order.index(e)] for e in range(n)]
    d_att, d_att_sib = call(
        functools.partial(cotangent_kernel, n),
        [shape(rows, head, dtype=F32)] * 2,
        *cots, *weights,
        scratch=[pltpu.VMEM((n, rows, feats), BF16)],
    )
    d_att_sib = swap(d_att_sib)
    mixed, root = call(
        functools.partial(combine_kernel, n, features),
        (shape(rows, width + head), shape(rows, rows, dtype=F32)),
        own_squares, d_att, d_att_sib, *parts,
    )
    w_sib = swap(after(w, mixed))
    mixed = [mixed] + [to_plane(mixed, e) for e in range(1, n)]
    attended, d_proj = call(
        functools.partial(attention_kernel, n, features),
        (shape(rows, head + STAT), shape(tokens, width)),
        block_mask, *mixed,
        smem=(0,),
        scratch=[
            pltpu.VMEM((tokens, width + head), BF16),
            pltpu.VMEM((tokens, tokens), BF16),
            pltpu.VMEM((tokens, tokens), BF16),
        ],
    )
    d_proj_sib, attended_sib = lax.optimization_barrier((swap(d_proj), swap(attended)))
    back = call(back_own_kernel, shape(tokens, feats, dtype=F32), d_proj, w)
    grads = call(
        functools.partial(back_sum_kernel, n),
        [shape(rows, feats)] * n,
        back, d_proj_sib, w_sib,
        scratch=[pltpu.VMEM((tokens, feats), BF16)],
    )
    grads = [grads[0]] + [to_chip(grads[d], d) for d in range(1, n)]
    terms = call(
        functools.partial(term_kernel, n),
        [shape(rows, feats + STAT)] * n,
        attended, attended_sib, *weights,
        scratch=[pltpu.VMEM((n, rows, feats), BF16)],
    )
    terms = [terms[0]] + [to_chip(terms[d], d) for d in range(1, n)]
    grad = call(functools.partial(sum_kernel, n), shape(rows, feats), *grads)
    grad = move(grad, lambda c, k, z: (z, k, z ^ c))
    output, mean = call(
        functools.partial(finish_output_kernel, n),
        (shape(rows, feats), shape(rows, STAT, dtype=F32)),
        activations, *terms,
    )
    input_grad = call(
        finish_grad_kernel, shape(rows, feats),
        activations, gain, cotangent, root, mean, grad,
    )
    return (output, input_grad)


def solution(mesh):
    in_specs = (
        P("seq", "pipe"),
        P("pipe"),
        P("pipe", "seq", None),
        P("pipe", None, "seq"),
        P(),
        P("seq", "pipe"),
    )
    out_specs = (P("seq", "pipe"), P("seq", "pipe"))
    n = mesh.shape["seq"]
    assert mesh.shape["pipe"] == 2 * n
    return jax.shard_map(
        functools.partial(per_device, n),
        mesh=mesh,
        in_specs=in_specs,
        out_specs=out_specs,
        check_vma=False,
    )
```

```python
import functools
import math

import jax
import jax.numpy as jnp
from jax import lax
from jax.experimental import pallas as pl
from jax.experimental.pallas import tpu as pltpu
from jax.sharding import PartitionSpec as P

EPS = 1e-05
VMEM_LIMIT = 48 * 1024 * 1024
STAT = 128
AXES = ("pipe", "seq")
F32 = jnp.float32
BF16 = jnp.bfloat16


def place():
    pipe = lax.axis_index("pipe")
    return pipe // 2, pipe % 2, lax.axis_index("seq")


def nt(a, b):
    return lax.dot_general(a, b, (((1,), (1,)), ((), ())), preferred_element_type=F32)


def tn(a, b):
    return lax.dot_general(a, b, (((0,), (0,)), ((), ())), preferred_element_type=F32)


def nn(a, b):
    return jnp.dot(a, b, preferred_element_type=F32)


def span(index, size):
    if isinstance(index, int):
        return pl.ds(index * size, size)
    return pl.ds(pl.multiple_of(index * size, size), size)


def call(kernel, out_shape, *args, scratch=(), smem=()):
    specs = [
        pl.BlockSpec(memory_space=pltpu.SMEM if i in smem else pltpu.VMEM) for i in range(len(args))
    ]
    return pl.pallas_call(
        kernel,
        out_shape=out_shape,
        in_specs=specs,
        out_specs=jax.tree.map(lambda _: pl.BlockSpec(memory_space=pltpu.VMEM), out_shape),
        scratch_shapes=list(scratch),
        compiler_params=pltpu.CompilerParams(vmem_limit_bytes=VMEM_LIMIT),
    )(*args)


def shape(*dims, dtype=BF16):
    return jax.ShapeDtypeStruct(dims, dtype)


def stack_kernel(own, sib, out):
    _, core, _ = place()
    rows, feats = own.shape[0], out.shape[1]
    out[:rows, :] = own[:, span(core, feats)]
    out[rows:, :] = sib[:, span(core, feats)]


def rows_kernel(x, gain, out):
    rows, feats = x.shape
    out[:rows, :] = x[...]
    out[rows:, :] = jnp.broadcast_to(gain[...], (16, feats))


def gain_of(n, blocks, rows):
    chip, _, plane = place()
    chosen = jnp.zeros((8, blocks[0].shape[1]), F32)
    for d in range(n):
        lines = blocks[d][rows:, :].astype(F32)[:8]
        chosen += jnp.where(jnp.bitwise_xor(chip, d) == plane, lines, 0.0)
    return chosen[0:1, :]


def in_parts(value):
    first = value.astype(BF16)
    return first, (value - first.astype(F32)).astype(BF16)


def project(n, blocks, w, high, low, squares, rows):
    chip, _, _ = place()
    gain = gain_of(n, blocks, rows)
    ones = jnp.ones((8, blocks[0].shape[1]), BF16)
    for d in range(n):
        slot = jnp.bitwise_xor(chip, d)
        values = blocks[d][:rows, :].astype(F32)
        high[span(slot, rows), :], low[span(slot, rows), :] = in_parts(values * gain)
        square_high, square_low = in_parts(values * values)
        squares[slot] = nt(ones, square_high) + nt(ones, square_low)
    return nn(high[...], w) + nn(low[...], w)


def project_same_kernel(n, w, *refs):
    blocks, (out, squares, high, low) = refs[:n], refs[n:]
    _, core, _ = place()
    rows, feats = squares.shape[2], high.shape[1]
    out[...] = project(n, blocks, w[span(core, feats), :], high, low, squares, rows)


def project_kernel(n, w, same, same_squares, *refs):
    blocks, outs = refs[:n], refs[n : 2 * n]
    own_squares, high, low, squares = refs[2 * n :]
    _, core, _ = place()
    rows, feats = squares.shape[2], high.shape[1]
    width = w.shape[1]
    total = same[...] + project(n, blocks, w[span(1 - core, feats), :], high, low, squares, rows)
    line = lax.broadcasted_iota(jnp.int32, (16, rows), 0)
    outs[0][...] = total[:rows]
    own_squares[...] = same_squares[0] + squares[0]
    for e in range(1, n):
        outs[e][:rows, :] = total[e * rows : (e + 1) * rows].astype(BF16)
        sums = (same_squares[e] + squares[e])[0:1, :]
        first = sums.astype(BF16).astype(F32)
        stat = jnp.where(line == 0, first, jnp.where(line == 1, sums - first, 0.0))
        outs[e][rows:, :] = jnp.zeros((16, width), BF16)
        outs[e][rows:, :rows] = stat.astype(BF16)


def combine_kernel(n, features, squares, d_att, d_att_sib, *refs):
    parts, (out, root) = refs[:n], refs[n:]
    rows, width = parts[0].shape
    total = parts[0][...]
    sums = squares[0:1, :]
    for part in parts[1:]:
        total += part[:rows, :].astype(F32)
        sums += jnp.sum(part[rows:, :rows].astype(F32), axis=0, keepdims=True)
    scale = jnp.broadcast_to(lax.rsqrt(sums / features + EPS), (rows, rows)).T
    root[...] = scale
    out[:, :width] = (total * scale[:, :1]).astype(BF16)
    out[:, width:] = (d_att[...] + d_att_sib[...]).astype(BF16)


def cotangent_kernel(n, *refs):
    cots, weights, (own, sib, held) = refs[:n], refs[n : 2 * n], refs[2 * n :]
    chip, _, plane = place()
    turn = jnp.bitwise_xor(chip, plane)
    rows, head = own.shape
    for d in range(n):
        held[jnp.bitwise_xor(turn, d)] = cots[d][...]
    total = jnp.zeros((rows, 2 * head), F32)
    for e in range(n):
        total += nt(held[e], weights[e][...])
    own[...] = total[:, :head]
    sib[...] = total[:, head:]


def split_stat(column):
    high = column.astype(BF16).astype(F32)
    lane = lax.broadcasted_iota(jnp.int32, (column.shape[0], STAT), 1)
    return jnp.where(lane == 0, high, jnp.where(lane == 1, column - high, 0.0)).astype(BF16)


def attention_kernel(n, features, mask, *refs):
    blocks = refs[:n]
    attended_out, d_proj, held, probs_held, d_scores_held = refs[n:]
    _, _, plane = place()
    rows = blocks[0].shape[0]
    head = blocks[0].shape[1] // 4
    factor = 1.0 / math.sqrt(head)
    for e in range(n):
        held[e * rows : (e + 1) * rows, :] = blocks[e][...]
    key = held[:, head : 2 * head]
    value = held[:, 2 * head : 3 * head]
    column_block = lax.broadcasted_iota(jnp.int32, (1, n * rows), 1) // rows

    def bias(e):
        line = jnp.zeros((1, n * rows), F32)
        for other in range(n):
            entry = mask[jnp.bitwise_xor(plane, e), jnp.bitwise_xor(plane, other)]
            line = jnp.where(column_block == other, jnp.where(entry > 0, 0.0, -1e30), line)
        return jnp.broadcast_to(line, (rows, n * rows))

    together = min(n, 4)
    for first in range(0, n, together):
        at = slice(first * rows, (first + together) * rows)
        masked = jnp.concatenate([bias(first + e) for e in range(together)], axis=0)
        scores = nt(held[at, :head], key) * factor + masked
        expd = jnp.exp(scores - jnp.max(scores, axis=-1, keepdims=True))
        probs = expd * (1.0 / jnp.sum(expd, axis=-1, keepdims=True))
        d_probs = nt(held[at, 3 * head :], value)
        delta = jnp.sum(probs * d_probs, axis=-1, keepdims=True)
        d_scores = (probs * (d_probs - delta) * factor).astype(BF16)
        probs_held[at, :] = probs.astype(BF16)
        d_scores_held[at, :] = d_scores
        d_proj[at, :head] = nn(d_scores, key).astype(BF16)

    d_proj[:, head : 2 * head] = tn(d_scores_held[...], held[:, :head]).astype(BF16)
    d_proj[:, 2 * head :] = tn(probs_held[...], held[:, 3 * head :]).astype(BF16)
    attended_out[:, :head] = nn(probs_held[:rows, :], value).astype(BF16)
    products = d_proj[:rows, :].astype(F32) * held[:rows, : 3 * head].astype(F32)
    mean = jnp.sum(products, axis=1, keepdims=True) / features
    attended_out[:, head:] = split_stat(mean)


def back_own_kernel(d_proj, w, out):
    _, core, _ = place()
    out[...] = nt(d_proj[...], w[span(core, out.shape[1]), :])


def back_sum_kernel(n, own, d_proj, w, *refs):
    outs, held = refs[:n], refs[n]
    chip, core, _ = place()
    rows, feats = outs[0].shape
    held[...] = (own[...] + nt(d_proj[...], w[span(core, feats), :])).astype(BF16)
    for d in range(n):
        outs[d][...] = held[span(jnp.bitwise_xor(chip, d), rows), :]


def term_kernel(n, own, sib, *refs):
    weights, outs, held = refs[:n], refs[n : 2 * n], refs[2 * n]
    chip, _, plane = place()
    turn = jnp.bitwise_xor(chip, plane)
    head = weights[0].shape[0] // 2
    feats = weights[0].shape[1]
    for e in range(n):
        term = nn(own[:, :head], weights[e][:head, :]) + nn(sib[:, :head], weights[e][head:, :])
        held[jnp.bitwise_xor(turn, e)] = term.astype(BF16)
    rows = own.shape[0]
    means = jnp.sum(own[:, head:].astype(F32) + sib[:, head:].astype(F32), axis=1, keepdims=True)
    row = jnp.broadcast_to(means, (rows, rows)).T[:16]
    first = row.astype(BF16).astype(F32)
    line = lax.broadcasted_iota(jnp.int32, (16, rows), 0)
    stat = jnp.where(line == 0, first, jnp.where(line == 1, row - first, 0.0))
    for d in range(n):
        outs[d][:rows, :] = held[d]
        outs[d][rows:, :] = jnp.zeros((16, feats), BF16)
        outs[d][rows:, :rows] = stat.astype(BF16)


def sum_kernel(n, *refs):
    total = refs[0][...].astype(F32)
    for part in refs[1:n]:
        total += part[...].astype(F32)
    refs[n][...] = total.astype(BF16)


def finish_output_kernel(n, x, *refs):
    parts, (out, mean) = refs[:n], refs[n:]
    rows = x.shape[0]
    total = parts[0][...].astype(F32)
    for part in parts[1:]:
        total += part[...].astype(F32)
    out[...] = (x[...].astype(F32) + total[:rows]).astype(BF16)
    row = jnp.sum(total[rows:, :rows], axis=0, keepdims=True)
    mean[...] = jnp.broadcast_to(row, (rows, rows)).T


def finish_grad_kernel(x, gain, cot, root, mean, grad, out):
    scale = root[:, :1]
    shift = scale * mean[:, :1]
    centred = grad[...].astype(F32) * gain[...].astype(F32) - x[...].astype(F32) * shift
    out[...] = (cot[...].astype(F32) + scale * centred).astype(BF16)


def per_device(n, activations, norm_gain, w_qkv, w_out, block_mask, cotangent):
    rows, feats = activations.shape
    features = feats * 2 * n
    head = w_out.shape[1]
    width = w_qkv.shape[2]
    tokens = n * rows

    def move(value, target):
        pairs = []
        for chip in range(n):
            for core in range(2):
                for plane in range(n):
                    to_chip, to_core, to_plane = target(chip, core, plane)
                    pairs.append(((2 * chip + core) * n + plane, (2 * to_chip + to_core) * n + to_plane))
        return lax.ppermute(value, AXES, pairs)

    def swap(value):
        return move(value, lambda c, k, z: (c, 1 - k, z))

    def to_chip(value, d):
        return move(value, lambda c, k, z: (c ^ d, k, z))

    def to_plane(value, e):
        return move(value, lambda c, k, z: (c, k, z ^ e))

    def after(value, *earlier):
        return lax.optimization_barrier((value, *earlier))[0]

    w = w_qkv[0]
    wo = w_out[0]

    x_held = move(activations, lambda c, k, z: (z ^ c, k, c))
    gain = norm_gain.reshape(1, feats)
    wo_sib, w_sib = lax.optimization_barrier((swap(wo), swap(w)))
    cots = [cotangent] + [to_chip(cotangent, d) for d in range(1, n)]
    own = call(stack_kernel, shape(2 * head, feats), wo, wo_sib)
    order, step = [0, n // 2], n // 2
    far = to_plane(own, step)
    x_held, *cots = lax.optimization_barrier((x_held, *cots))
    x_held = call(rows_kernel, shape(rows + 16, feats), x_held, gain)
    x_same, x_sib = [x_held], [swap(x_held)]
    for d in range(1, n):
        block = to_chip(x_held, d)
        if d == min(1, n - 1):
            block, far = lax.optimization_barrier((block, far))
        x_same.append(block)
        x_sib.append(swap(block))
    weights = [own, far]
    while step > 1:
        step //= 2
        ready = [after(part, x_sib[0 if i == 0 else 0]) for i, part in enumerate(weights)]
        weights += [to_plane(part, step) for part in ready]
        order += [o ^ step for o in order]
    work = [pltpu.VMEM((tokens, feats), BF16)] * 2
    same, squares = call(
        functools.partial(project_same_kernel, n),
        (shape(tokens, width, dtype=F32), shape(n, 8, rows, dtype=F32)),
        w, *x_same,
        scratch=work,
    )
    *parts, own_squares = call(
        functools.partial(project_kernel, n),
        [shape(rows, width, dtype=F32)]
        + [shape(rows + 16, width)] * (n - 1)
        + [shape(8, rows, dtype=F32)],
        w, same, squares, *x_sib,
        scratch=work + [pltpu.VMEM((n, 8, rows), F32)],
    )
    parts = [parts[0]] + [to_plane(parts[e], e) for e in range(1, n)]

    weights = [weights[order.index(e)] for e in range(n)]
    d_att, d_att_sib = call(
        functools.partial(cotangent_kernel, n),
        [shape(rows, head, dtype=F32)] * 2,
        *cots, *weights,
        scratch=[pltpu.VMEM((n, rows, feats), BF16)],
    )
    d_att_sib = swap(d_att_sib)
    mixed, root = call(
        functools.partial(combine_kernel, n, features),
        (shape(rows, width + head), shape(rows, rows, dtype=F32)),
        own_squares, d_att, d_att_sib, parts[0], *parts[:0:-1],
    )
    mixed = [mixed] + [to_plane(mixed, e) for e in range(1, n)]
    attended, d_proj = call(
        functools.partial(attention_kernel, n, features),
        (shape(rows, head + STAT), shape(tokens, width)),
        block_mask, *mixed,
        smem=(0,),
        scratch=[
            pltpu.VMEM((tokens, width + head), BF16),
            pltpu.VMEM((tokens, tokens), BF16),
            pltpu.VMEM((tokens, tokens), BF16),
        ],
    )
    d_proj_sib, attended_sib = lax.optimization_barrier((swap(d_proj), swap(attended)))
    back = call(back_own_kernel, shape(tokens, feats, dtype=F32), d_proj, w)
    grads = call(
        functools.partial(back_sum_kernel, n),
        [shape(rows, feats)] * n,
        back, d_proj_sib, w_sib,
        scratch=[pltpu.VMEM((tokens, feats), BF16)],
    )
    grads = [grads[0]] + [to_chip(grads[d], d) for d in range(1, n)]
    terms = call(
        functools.partial(term_kernel, n),
        [shape(rows + 16, feats)] * n,
        attended, attended_sib, *weights,
        scratch=[pltpu.VMEM((n, rows, feats), BF16)],
    )
    terms = [terms[0]] + [to_chip(terms[d], d) for d in range(1, n)]
    grad = call(functools.partial(sum_kernel, n), shape(rows, feats), *grads)
    grad = move(grad, lambda c, k, z: (z, k, z ^ c))
    output, mean = call(
        functools.partial(finish_output_kernel, n),
        (shape(rows, feats), shape(rows, rows, dtype=F32)),
        activations, *terms,
    )
    input_grad = call(
        finish_grad_kernel, shape(rows, feats),
        activations, gain, cotangent, root, mean, grad,
    )
    return (output, input_grad)


def solution(mesh):
    in_specs = (
        P("seq", "pipe"),
        P("pipe"),
        P("pipe", "seq", None),
        P("pipe", None, "seq"),
        P(),
        P("seq", "pipe"),
    )
    out_specs = (P("seq", "pipe"), P("seq", "pipe"))
    n = mesh.shape["seq"]
    assert mesh.shape["pipe"] == 2 * n
    return jax.shard_map(
        functools.partial(per_device, n),
        mesh=mesh,
        in_specs=in_specs,
        out_specs=out_specs,
        check_vma=False,
    )
```

```python
import functools
import math

import jax
import jax.numpy as jnp
from jax import lax
from jax.experimental import pallas as pl
from jax.experimental.pallas import tpu as pltpu
from jax.sharding import PartitionSpec as P

EPS = 1e-05
VMEM_LIMIT = 48 * 1024 * 1024
STAT = 128
AXES = ("pipe", "seq")
F32 = jnp.float32
BF16 = jnp.bfloat16


def place():
    pipe = lax.axis_index("pipe")
    return pipe // 2, pipe % 2, lax.axis_index("seq")


def nt(a, b):
    return lax.dot_general(a, b, (((1,), (1,)), ((), ())), preferred_element_type=F32)


def tn(a, b):
    return lax.dot_general(a, b, (((0,), (0,)), ((), ())), preferred_element_type=F32)


def nn(a, b):
    return jnp.dot(a, b, preferred_element_type=F32)


def span(index, size):
    if isinstance(index, int):
        return pl.ds(index * size, size)
    return pl.ds(pl.multiple_of(index * size, size), size)


def call(kernel, out_shape, *args, scratch=(), smem=()):
    specs = [
        pl.BlockSpec(memory_space=pltpu.SMEM if i in smem else pltpu.VMEM) for i in range(len(args))
    ]
    return pl.pallas_call(
        kernel,
        out_shape=out_shape,
        in_specs=specs,
        out_specs=jax.tree.map(lambda _: pl.BlockSpec(memory_space=pltpu.VMEM), out_shape),
        scratch_shapes=list(scratch),
        compiler_params=pltpu.CompilerParams(vmem_limit_bytes=VMEM_LIMIT),
    )(*args)


def shape(*dims, dtype=BF16):
    return jax.ShapeDtypeStruct(dims, dtype)


def stack_kernel(own, sib, out):
    _, core, _ = place()
    rows, feats = own.shape[0], out.shape[1]
    out[:rows, :] = own[:, span(core, feats)]
    out[rows:, :] = sib[:, span(core, feats)]


def rows_kernel(x, gain, out):
    rows, feats = x.shape
    out[:rows, :] = x[...]
    out[rows:, :] = jnp.broadcast_to(gain[...], (16, feats))


def gain_of(n, blocks, rows):
    chip, _, plane = place()
    chosen = jnp.zeros((8, blocks[0].shape[1]), F32)
    for d in range(n):
        lines = blocks[d][rows:, :].astype(F32)[:8]
        chosen += jnp.where(jnp.bitwise_xor(chip, d) == plane, lines, 0.0)
    return chosen[0:1, :]


def in_parts(value):
    first = value.astype(BF16)
    return first, (value - first.astype(F32)).astype(BF16)


def project(n, blocks, w, high, low, squares, rows):
    chip, _, _ = place()
    gain = gain_of(n, blocks, rows)
    ones = jnp.ones((8, blocks[0].shape[1]), BF16)
    for d in range(n):
        slot = jnp.bitwise_xor(chip, d)
        values = blocks[d][:rows, :].astype(F32)
        high[span(slot, rows), :], low[span(slot, rows), :] = in_parts(values * gain)
        square_high, square_low = in_parts(values * values)
        squares[slot] = nt(ones, square_high) + nt(ones, square_low)
    return nn(high[...], w) + nn(low[...], w)


def project_same_kernel(n, w, *refs):
    blocks, (out, squares, high, low) = refs[:n], refs[n:]
    _, core, _ = place()
    rows, feats = squares.shape[2], high.shape[1]
    out[...] = project(n, blocks, w[span(core, feats), :], high, low, squares, rows)


def project_kernel(n, w, same, same_squares, *refs):
    blocks, outs = refs[:n], refs[n : 2 * n]
    own_squares, high, low, squares = refs[2 * n :]
    _, core, _ = place()
    rows, feats = squares.shape[2], high.shape[1]
    width = w.shape[1]
    total = same[...] + project(n, blocks, w[span(1 - core, feats), :], high, low, squares, rows)
    line = lax.broadcasted_iota(jnp.int32, (16, rows), 0)
    outs[0][...] = total[:rows]
    own_squares[...] = same_squares[0] + squares[0]
    for e in range(1, n):
        outs[e][:rows, :] = total[e * rows : (e + 1) * rows].astype(BF16)
        sums = (same_squares[e] + squares[e])[0:1, :]
        first = sums.astype(BF16).astype(F32)
        stat = jnp.where(line == 0, first, jnp.where(line == 1, sums - first, 0.0))
        outs[e][rows:, :] = jnp.zeros((16, width), BF16)
        outs[e][rows:, :rows] = stat.astype(BF16)


def combine_kernel(n, features, squares, d_att, d_att_sib, *refs):
    parts, (out, first, second, root) = refs[:n], refs[n:]
    rows, width = parts[0].shape
    total = parts[0][...]
    sums = squares[0:1, :]
    for part in parts[1:]:
        total += part[:rows, :].astype(F32)
        sums += jnp.sum(part[rows:, :rows].astype(F32), axis=0, keepdims=True)
    scale = jnp.broadcast_to(lax.rsqrt(sums / features + EPS), (rows, rows)).T
    root[...] = scale
    out[:, :width] = (total * scale[:, :1]).astype(BF16)
    out[:, width:] = (d_att[...] + d_att_sib[...]).astype(BF16)
    first[...] = out[: rows // 2, :]
    second[...] = out[rows // 2 :, :]


def cotangent_kernel(n, *refs):
    cots, weights, (own, sib, held) = refs[:n], refs[n : 2 * n], refs[2 * n :]
    chip, _, plane = place()
    turn = jnp.bitwise_xor(chip, plane)
    rows, head = own.shape
    for d in range(n):
        held[jnp.bitwise_xor(turn, d)] = cots[d][...]
    total = jnp.zeros((rows, 2 * head), F32)
    for e in range(n):
        total += nt(held[e], weights[e][...])
    own[...] = total[:, :head]
    sib[...] = total[:, head:]


def split_stat(column):
    high = column.astype(BF16).astype(F32)
    lane = lax.broadcasted_iota(jnp.int32, (column.shape[0], STAT), 1)
    return jnp.where(lane == 0, high, jnp.where(lane == 1, column - high, 0.0)).astype(BF16)


def attention_kernel(n, rows, features, starts, mask, *refs):
    blocks = refs[: len(starts)]
    attended_out, d_proj, held, probs_held, d_scores_held = refs[len(starts) :]
    _, _, plane = place()
    head = blocks[0].shape[1] // 4
    factor = 1.0 / math.sqrt(head)
    for start, block in zip(starts, blocks):
        held[start : start + block.shape[0], :] = block[...]
    key = held[:, head : 2 * head]
    value = held[:, 2 * head : 3 * head]
    column_block = lax.broadcasted_iota(jnp.int32, (1, n * rows), 1) // rows

    def bias(e):
        line = jnp.zeros((1, n * rows), F32)
        for other in range(n):
            entry = mask[jnp.bitwise_xor(plane, e), jnp.bitwise_xor(plane, other)]
            line = jnp.where(column_block == other, jnp.where(entry > 0, 0.0, -1e30), line)
        return jnp.broadcast_to(line, (rows, n * rows))

    together = min(n, 4)
    for first in range(0, n, together):
        at = slice(first * rows, (first + together) * rows)
        masked = jnp.concatenate([bias(first + e) for e in range(together)], axis=0)
        scores = nt(held[at, :head], key) * factor + masked
        expd = jnp.exp(scores - jnp.max(scores, axis=-1, keepdims=True))
        probs = expd * (1.0 / jnp.sum(expd, axis=-1, keepdims=True))
        d_probs = nt(held[at, 3 * head :], value)
        delta = jnp.sum(probs * d_probs, axis=-1, keepdims=True)
        d_scores = (probs * (d_probs - delta) * factor).astype(BF16)
        probs_held[at, :] = probs.astype(BF16)
        d_scores_held[at, :] = d_scores
        d_proj[at, :head] = nn(d_scores, key).astype(BF16)

    d_proj[:, head : 2 * head] = tn(d_scores_held[...], held[:, :head]).astype(BF16)
    d_proj[:, 2 * head :] = tn(probs_held[...], held[:, 3 * head :]).astype(BF16)
    attended_out[:, :head] = nn(probs_held[:rows, :], value).astype(BF16)
    products = d_proj[:rows, :].astype(F32) * held[:rows, : 3 * head].astype(F32)
    mean = jnp.sum(products, axis=1, keepdims=True) / features
    attended_out[:, head:] = split_stat(mean)


def back_own_kernel(d_proj, w, out):
    _, core, _ = place()
    out[...] = nt(d_proj[...], w[span(core, out.shape[1]), :])


def back_sum_kernel(n, own, d_proj, w, *refs):
    outs, held = refs[:n], refs[n]
    chip, core, _ = place()
    rows, feats = outs[0].shape
    held[...] = (own[...] + nt(d_proj[...], w[span(core, feats), :])).astype(BF16)
    for d in range(n):
        outs[d][...] = held[span(jnp.bitwise_xor(chip, d), rows), :]


def term_kernel(n, own, sib, *refs):
    weights, outs, held = refs[:n], refs[n : 2 * n], refs[2 * n]
    chip, _, plane = place()
    turn = jnp.bitwise_xor(chip, plane)
    head = weights[0].shape[0] // 2
    feats = weights[0].shape[1]
    for e in range(n):
        term = nn(own[:, :head], weights[e][:head, :]) + nn(sib[:, :head], weights[e][head:, :])
        held[jnp.bitwise_xor(turn, e)] = term.astype(BF16)
    rows = own.shape[0]
    means = jnp.sum(own[:, head:].astype(F32) + sib[:, head:].astype(F32), axis=1, keepdims=True)
    row = jnp.broadcast_to(means, (rows, rows)).T[:16]
    first = row.astype(BF16).astype(F32)
    line = lax.broadcasted_iota(jnp.int32, (16, rows), 0)
    stat = jnp.where(line == 0, first, jnp.where(line == 1, row - first, 0.0))
    for d in range(n):
        outs[d][:rows, :] = held[d]
        outs[d][rows:, :] = jnp.zeros((16, feats), BF16)
        outs[d][rows:, :rows] = stat.astype(BF16)


def sum_kernel(n, *refs):
    total = refs[0][...].astype(F32)
    for part in refs[1:n]:
        total += part[...].astype(F32)
    refs[n][...] = total.astype(BF16)


def finish_output_kernel(n, x, *refs):
    parts, (out, mean) = refs[:n], refs[n:]
    rows = x.shape[0]
    total = parts[0][...].astype(F32)
    for part in parts[1:]:
        total += part[...].astype(F32)
    out[...] = (x[...].astype(F32) + total[:rows]).astype(BF16)
    row = jnp.sum(total[rows:, :rows], axis=0, keepdims=True)
    mean[...] = jnp.broadcast_to(row, (rows, rows)).T


def finish_grad_kernel(x, gain, cot, root, mean, grad, out):
    scale = root[:, :1]
    shift = scale * mean[:, :1]
    centred = grad[...].astype(F32) * gain[...].astype(F32) - x[...].astype(F32) * shift
    out[...] = (cot[...].astype(F32) + scale * centred).astype(BF16)


def per_device(n, activations, norm_gain, w_qkv, w_out, block_mask, cotangent):
    rows, feats = activations.shape
    features = feats * 2 * n
    head = w_out.shape[1]
    width = w_qkv.shape[2]
    tokens = n * rows

    def move(value, target):
        pairs = []
        for chip in range(n):
            for core in range(2):
                for plane in range(n):
                    to_chip, to_core, to_plane = target(chip, core, plane)
                    pairs.append(((2 * chip + core) * n + plane, (2 * to_chip + to_core) * n + to_plane))
        return lax.ppermute(value, AXES, pairs)

    def swap(value):
        return move(value, lambda c, k, z: (c, 1 - k, z))

    def to_chip(value, d):
        return move(value, lambda c, k, z: (c ^ d, k, z))

    def to_plane(value, e):
        return move(value, lambda c, k, z: (c, k, z ^ e))

    def after(value, *earlier):
        return lax.optimization_barrier((value, *earlier))[0]

    w = w_qkv[0]
    wo = w_out[0]

    x_held = move(activations, lambda c, k, z: (z ^ c, k, c))
    gain = norm_gain.reshape(1, feats)
    wo_sib, w_sib = lax.optimization_barrier((swap(wo), swap(w)))
    cots = [cotangent] + [to_chip(cotangent, d) for d in range(1, n)]
    own = call(stack_kernel, shape(2 * head, feats), wo, wo_sib)
    order, step = [0, n // 2], n // 2
    far = to_plane(own, step)
    x_held, *cots = lax.optimization_barrier((x_held, *cots))
    x_held = call(rows_kernel, shape(rows + 16, feats), x_held, gain)
    x_same, x_sib = [x_held], [swap(x_held)]
    for d in range(1, n):
        block = to_chip(x_held, d)
        if d == min(1, n - 1):
            block, far = lax.optimization_barrier((block, far))
        x_same.append(block)
        x_sib.append(swap(block))
    weights = [own, far]
    while step > 1:
        step //= 2
        ready = [after(part, x_sib[0 if i == 0 else 0]) for i, part in enumerate(weights)]
        weights += [to_plane(part, step) for part in ready]
        order += [o ^ step for o in order]
    work = [pltpu.VMEM((tokens, feats), BF16)] * 2
    same, squares = call(
        functools.partial(project_same_kernel, n),
        (shape(tokens, width, dtype=F32), shape(n, 8, rows, dtype=F32)),
        w, *x_same,
        scratch=work,
    )
    *parts, own_squares = call(
        functools.partial(project_kernel, n),
        [shape(rows, width, dtype=F32)]
        + [shape(rows + 16, width)] * (n - 1)
        + [shape(8, rows, dtype=F32)],
        w, same, squares, *x_sib,
        scratch=work + [pltpu.VMEM((n, 8, rows), F32)],
    )
    parts = [parts[0]] + [to_plane(parts[e], e) for e in range(1, n)]

    weights = [weights[order.index(e)] for e in range(n)]
    d_att, d_att_sib = call(
        functools.partial(cotangent_kernel, n),
        [shape(rows, head, dtype=F32)] * 2,
        *cots, *weights,
        scratch=[pltpu.VMEM((n, rows, feats), BF16)],
    )
    d_att_sib = swap(d_att_sib)
    mixed, first, second, root = call(
        functools.partial(combine_kernel, n, features),
        (shape(rows, width + head),)
        + (shape(rows // 2, width + head),) * 2
        + (shape(rows, rows, dtype=F32),),
        own_squares, d_att, d_att_sib, parts[0], *parts[:0:-1],
    )
    if n == 4:
        near = [to_plane(first, 1), to_plane(second, 1)]
        far = [to_plane(first, 2), to_plane(second, 2)]
        third = [to_plane(first, 3), to_plane(far[1], 1)]
        mixed = [mixed, *near, *far, *third]
        starts = [0, rows, 3 * rows // 2, 2 * rows, 5 * rows // 2, 3 * rows, 7 * rows // 2]
    else:
        mixed = [mixed] + [to_plane(mixed, e) for e in range(1, n)]
        starts = [e * rows for e in range(n)]
    attended, d_proj = call(
        functools.partial(attention_kernel, n, rows, features, starts),
        (shape(rows, head + STAT), shape(tokens, width)),
        block_mask, *mixed,
        smem=(0,),
        scratch=[
            pltpu.VMEM((tokens, width + head), BF16),
            pltpu.VMEM((tokens, tokens), BF16),
            pltpu.VMEM((tokens, tokens), BF16),
        ],
    )
    d_proj_sib, attended_sib = lax.optimization_barrier((swap(d_proj), swap(attended)))
    back = call(back_own_kernel, shape(tokens, feats, dtype=F32), d_proj, w)
    grads = call(
        functools.partial(back_sum_kernel, n),
        [shape(rows, feats)] * n,
        back, d_proj_sib, w_sib,
        scratch=[pltpu.VMEM((tokens, feats), BF16)],
    )
    grads = [grads[0]] + [to_chip(grads[d], d) for d in range(1, n)]
    terms = call(
        functools.partial(term_kernel, n),
        [shape(rows + 16, feats)] * n,
        attended, attended_sib, *weights,
        scratch=[pltpu.VMEM((n, rows, feats), BF16)],
    )
    terms = [terms[0]] + [to_chip(terms[d], d) for d in range(1, n)]
    grad = call(functools.partial(sum_kernel, n), shape(rows, feats), *grads)
    grad = move(grad, lambda c, k, z: (z, k, z ^ c))
    output, mean = call(
        functools.partial(finish_output_kernel, n),
        (shape(rows, feats), shape(rows, rows, dtype=F32)),
        activations, *terms,
    )
    input_grad = call(
        finish_grad_kernel, shape(rows, feats),
        activations, gain, cotangent, root, mean, grad,
    )
    return (output, input_grad)


def solution(mesh):
    in_specs = (
        P("seq", "pipe"),
        P("pipe"),
        P("pipe", "seq", None),
        P("pipe", None, "seq"),
        P(),
        P("seq", "pipe"),
    )
    out_specs = (P("seq", "pipe"), P("seq", "pipe"))
    n = mesh.shape["seq"]
    assert mesh.shape["pipe"] == 2 * n
    return jax.shard_map(
        functools.partial(per_device, n),
        mesh=mesh,
        in_specs=in_specs,
        out_specs=out_specs,
        check_vma=False,
    )
```
